32 devices in a mesh: slab: 8 (over z, core), pencil: 4 (over y, x).
Axes of the slice: x: 2, y: 2, z: 4, core: 2. Of those that a mesh axis runs over, the one named last changes fastest.
Arguments:
- fractions: float32 [3, 524288], P(None, ('slab', 'pencil')), may hold values from 0 to 1
- cell_index: int32 [3, 524288], P(None, ('slab', 'pencil')), may hold values from 0 to 255, as said below
- weights: bfloat16 [4, 524288], P(None, ('slab', 'pencil')), may hold values from -6 to 6
- counts: int32 [32, 32, 32], P(('slab', 'pencil')), may hold values from 0 to 16, as said below
- smoothing: float32 [4], replicated, may hold values from 1 to 256
- bias_values: float32 [4], replicated, may hold values from 0.5 to 1.5
- observed: float32 [8, 1024, 1024], P('slab', 'pencil'), may hold values from -6 to 6
- precision: float32 [8, 1024, 1024], P('slab', 'pencil'), may hold values from 0.25 to 4
Outputs:
- particle_grads: float32 [7, 524288], P(None, ('slab', 'pencil'))
- model_field: bfloat16 [8, 1024, 1024], P('slab', 'pencil')
The draws below stay inside these ranges and needn't reach their ends.
Inputs may be any that keep to these rules, and one draw needn't show every extreme that they name: counts[s, t, b] is how many of the 16 slots that device s holds for z block b of tile t are live (the first ones); some tile gets 16 for every block from every device. `cell_index`: row 0 is below 1, row 1 below 256, row 2 below 32.
All inputs are finite; a program needn't handle non-finite values.
Results may differ from the reference program's by a relative error of at most 0.0074.
Values may be sent and summed in bfloat16 or wider, within the bound.
A program may use at most 192 MiB of HBM per device.

```python
import math
import jax
import jax.numpy as jnp
from jax import lax

TX = 1
NY = 1024
NZ = 1024
C = 4
ZB = 32
PART_DEV = 16384
TILES = 32
NX = 8
TY = 256
ZBLK = 32
CAP = 16
N_PENCIL = 4


def draw_cell_index(key, part):
    key_x, key_y, key_z = jax.random.split(key, 3)
    slot_total = TILES * PART_DEV
    along_x = jax.random.randint(key_x, (1, slot_total), 0, TX)
    along_y = jax.random.randint(key_y, (1, slot_total), 0, TY)
    along_z = jax.random.randint(key_z, (1, slot_total), 0, ZB)
    return jnp.concatenate([along_x, along_y, along_z], axis=0).astype(jnp.int32)


def draw_counts(key, part):
    key_light, key_heavy, key_forced = jax.random.split(key, 3)
    light_load = jax.random.randint(key_light, (TILES, TILES, ZBLK), 0, CAP)
    picked = jax.random.randint(key_heavy, (TILES,), 0, 8) == 0
    forced = jnp.arange(TILES) == jax.random.randint(key_forced, (), 0, TILES)
    heavy_tile = jnp.logical_or(picked, forced)
    return jnp.where(heavy_tile[None, :, None], CAP, light_load).astype(jnp.int32)


def draw_smoothing(key, part):
    key_stratum, key_jitter = jax.random.split(key, 2)
    stratum = jax.random.permutation(key_stratum, C).astype(jnp.float32)
    jitter = jax.random.uniform(key_jitter, (C,), jnp.float32)
    position = (stratum + jitter) / C
    return jnp.exp(position * math.log(NY / 4.0)).astype(jnp.float32)


def draw_observed(key, part):
    key_rough = jax.random.fold_in(key, 0)
    extent_all = (NX, NZ, NY)
    return jnp.clip(jax.random.normal(key_rough, extent_all, jnp.float32), -6.0, 6.0)


def shard_levels(own_key, dims, cuts, least, top_value):
    loudness = 1.0
    for axis_at, shards_of in cuts:
        steps = jax.random.uniform(jax.random.fold_in(jax.random.fold_in(own_key, 6), axis_at), (shards_of,), jnp.float32, least / len(cuts), top_value / len(cuts))
        loudness = loudness * jnp.repeat(jnp.exp(steps), dims[axis_at] // shards_of).reshape((-1,) + (1,) * (len(dims) - 1 - axis_at))
    return loudness


def scatter_about(rng, dims, width, most, cuts=(), kind=jnp.bfloat16):
    drawn = width * jax.random.normal(rng, dims, jnp.float32)
    if cuts:
        drawn = drawn * shard_levels(rng, dims, cuts, -0.22, 0.18)
    return jnp.clip(drawn, -most, most).astype(kind)


def setup_inputs(seed: int = 0) -> dict:
    key_of = jax.random.split(jax.random.key(seed), 9)
    fractions = jnp.clip(1.0 * jax.random.uniform(key_of[0], (3, TILES * PART_DEV), jnp.float32) ** shard_levels(key_of[0], (3, TILES * PART_DEV), ((1, 32),), -0.2, 0.2), 0.0, 1.0)
    cell_index = draw_cell_index(jax.random.fold_in(key_of[8], 71), 0)
    weights = scatter_about(key_of[2], (C, TILES * PART_DEV), 1.0, 6.0, ((1, 32),))
    counts = draw_counts(jax.random.fold_in(key_of[8], 71), 0)
    smoothing = draw_smoothing(jax.random.fold_in(key_of[8], 71), 0)
    bias_values = jnp.clip(jax.random.uniform(key_of[5], (C,), jnp.float32, 0.5, 1.5), 0.5, 1.5)
    observed = draw_observed(jax.random.fold_in(key_of[8], 71), 0)
    precision = jnp.clip(jnp.exp(math.log(4.0) - 2.7725887 * jax.random.uniform(key_of[7], (NX, NZ, NY), jnp.float32) ** shard_levels(key_of[7], (NX, NZ, NY), ((0, 8), (1, 4)), -0.2, 0.2)), 0.25, 4.0)
    return {"fractions": fractions, "cell_index": cell_index, "weights": weights, "counts": counts, "smoothing": smoothing, "bias_values": bias_values, "observed": observed, "precision": precision}


def rounded(values):
    return lax.optimization_barrier(values.astype(jnp.bfloat16)).astype(jnp.float32)

def kernel_matrix(breadth, extent):
    places = jnp.arange(extent, dtype=jnp.int32)
    distance = jnp.abs(places[:, None] - places[None, :])
    distance = jnp.minimum(distance, extent - distance).astype(jnp.float32)
    profile = jnp.exp(-distance * distance / (2.0 * breadth * breadth)) / jnp.sqrt(breadth)
    return (profile + jnp.where(distance == 0.0, 1.0, 0.0)).astype(jnp.bfloat16)

def cloud_table(fraction):
    falling = fraction < 0.5
    weights_1d = [jnp.maximum(0.5 - fraction, 0.0), 1.0 - jnp.abs(fraction - 0.5), jnp.maximum(fraction - 0.5, 0.0)]
    slopes_1d = [jnp.where(falling, -1.0, 0.0), jnp.where(falling, 1.0, -1.0), jnp.where(falling, 0.0, 1.0)]
    return (weights_1d, slopes_1d)

def reference(fractions, cell_index, weights, counts, smoothing, bias_values, observed, precision):
    slot_total = TILES * PART_DEV
    slot_index = jnp.arange(slot_total, dtype=jnp.int32)
    source = slot_index // PART_DEV
    on_device = slot_index % PART_DEV
    tile_index = on_device // (ZBLK * CAP)
    block_index = on_device // CAP % ZBLK
    slot_rank = on_device % CAP
    live_mask = (slot_rank < counts[source, tile_index, block_index]).astype(jnp.float32)
    masses = weights.astype(jnp.float32) * live_mask[None, :]
    grid_x = tile_index // N_PENCIL * TX + cell_index[0]
    grid_y = tile_index % N_PENCIL * TY + cell_index[1]
    grid_z = block_index * ZB + cell_index[2]
    weight_x, slope_x = cloud_table(fractions[0])
    weight_y, slope_y = cloud_table(fractions[1])
    weight_z, slope_z = cloud_table(fractions[2])
    cells_x = [(grid_x + step - 1) % NX for step in range(3)]
    cells_y = [(grid_y + step - 1) % NY for step in range(3)]
    cells_z = [(grid_z + step - 1) % NZ for step in range(3)]
    highest = lax.Precision.HIGHEST
    model_values = jnp.zeros((NX, NZ, NY), jnp.float32)
    for channel in range(C):
        flat_field = jnp.zeros((NX * NY * NZ,), jnp.float32)
        for step_x in range(3):
            for step_y in range(3):
                plane_w = rounded(weight_x[step_x] * weight_y[step_y])
                for step_z in range(3):
                    column_w = rounded(masses[channel] * weight_z[step_z])
                    target = (cells_x[step_x] * NY + cells_y[step_y]) * NZ + cells_z[step_z]
                    flat_field = flat_field.at[target].add(plane_w * column_w)
        density = flat_field.reshape(NX, NY, NZ).astype(jnp.bfloat16)
        kernel_y = kernel_matrix(smoothing[channel], NY).astype(jnp.float32)
        kernel_z = kernel_matrix(smoothing[channel], NZ).astype(jnp.float32)
        smooth_z = jnp.einsum('xyz,zw->xyw', density.astype(jnp.float32), kernel_z, precision=highest).astype(jnp.bfloat16)
        model_values = model_values + bias_values[channel] * jnp.einsum('xyz,yw->xzw', smooth_z.astype(jnp.float32), kernel_y, precision=highest)
    model_field = model_values.astype(jnp.bfloat16)
    pull_field = rounded(precision * (model_values - observed))
    grad_rows = []
    grad_x = jnp.zeros((slot_total,), jnp.float32)
    grad_y = jnp.zeros((slot_total,), jnp.float32)
    grad_z = jnp.zeros((slot_total,), jnp.float32)
    for channel in range(C):
        kernel_y = kernel_matrix(smoothing[channel], NY).astype(jnp.float32)
        kernel_z = kernel_matrix(smoothing[channel], NZ).astype(jnp.float32)
        returned_y = rounded(bias_values[channel] * jnp.einsum('xzy,yw->xwz', pull_field, kernel_y, precision=highest))
        adjoint = rounded(jnp.einsum('xyz,zw->xyw', returned_y, kernel_z, precision=highest)).reshape(-1)
        grad_mass = jnp.zeros((slot_total,), jnp.float32)
        for step_x in range(3):
            for step_y in range(3):
                plane_w = rounded(weight_x[step_x] * weight_y[step_y])
                slope_xw = rounded(slope_x[step_x] * weight_y[step_y])
                slope_yw = rounded(weight_x[step_x] * slope_y[step_y])
                for step_z in range(3):
                    target = (cells_x[step_x] * NY + cells_y[step_y]) * NZ + cells_z[step_z]
                    sampled = adjoint[target]
                    grad_mass = grad_mass + plane_w * sampled * weight_z[step_z]
                    grad_x = grad_x + masses[channel] * slope_xw * sampled * weight_z[step_z]
                    grad_y = grad_y + masses[channel] * slope_yw * sampled * weight_z[step_z]
                    grad_z = grad_z + masses[channel] * plane_w * sampled * slope_z[step_z]
        grad_rows.append(grad_mass)
    particle_grads = jnp.stack(grad_rows + [grad_x, grad_y, grad_z]) * live_mask[None, :]
    return (particle_grads, model_field)
```

```python
import functools

import jax
import jax.numpy as jnp
from jax import lax
from jax.experimental import pallas as pl
from jax.experimental.pallas import tpu as pltpu
from jax.sharding import PartitionSpec as P

NY = 1024
NZ = 1024
ZB = 32
PART_DEV = 16384
HALO_ROWS = 8
NT = (((1,), (1,)), ((), ()))
NN = (((1,), (0,)), ((), ()))


def shifted(value, axis, step):
    count = lax.axis_size(axis)
    return lax.ppermute(value, axis, [(i, (i + step) % count) for i in range(count)])


def kernel_matrix(breadth, extent):
    places = jnp.arange(extent, dtype=jnp.int32)
    distance = jnp.abs(places[:, None] - places[None, :])
    distance = jnp.minimum(distance, extent - distance).astype(jnp.float32)
    profile = jnp.exp(-distance * distance / (2.0 * breadth * breadth)) / jnp.sqrt(breadth)
    return (profile + jnp.where(distance == 0.0, 1.0, 0.0)).astype(jnp.bfloat16)


def y_places(tile_y, slots):
    main = lax.broadcasted_iota(jnp.int32, (tile_y, slots), 0).astype(jnp.float32)
    rim = lax.broadcasted_iota(jnp.int32, (HALO_ROWS, slots), 0)
    rim = jnp.where(rim == 0, -1.0, jnp.where(rim == 1, float(tile_y), -1000.0))
    return jnp.concatenate([main, rim], axis=0)


def z_places(rows, below, slots):
    return (lax.broadcasted_iota(jnp.int32, (rows, slots), 0) - below).astype(jnp.float32)


def hat(places, position):
    return jnp.maximum(1.0 - jnp.abs(places - position), 0.0)


def step_pair(places, lower):
    relative = places - lower
    return jnp.where(relative == 1.0, 1.0, jnp.where(relative == 0.0, -1.0, 0.0))


def x_weight(group, gx):
    if group == 0:
        return 1.0 - jnp.abs(gx)
    return jnp.maximum(gx if group == 1 else -gx, 0.0)


def x_slope(group, gx):
    falling = gx < 0.0
    if group == 0:
        return jnp.where(falling, 1.0, -1.0)
    if group == 1:
        return jnp.where(falling, 0.0, 1.0)
    return jnp.where(falling, -1.0, 0.0)


def deposit_kernel(tile_y, channels, own_ref, prev_ref, next_ref, main_ref, rim_ref, total):
    block = pl.program_id(0)
    rows = ZB + 8
    slots = own_ref.shape[2]

    @pl.when(block == 0)
    def _():
        total[...] = jnp.zeros_like(total)

    places = y_places(tile_y, slots)
    zs = z_places(rows, 1, slots)
    columns = []
    planes = []
    for group, ref in enumerate((own_ref, prev_ref, next_ref)):
        record = ref[0]
        gx, gy, gz, iy, iz = (record[i : i + 1] for i in range(5))
        along_z = hat(zs, iz + gz) * x_weight(group, gx)
        columns.append(
            jnp.concatenate(
                [along_z * record[5 + c : 6 + c] for c in range(channels)], axis=0
            ).astype(jnp.bfloat16)
        )
        planes.append(hat(places, iy + gy).astype(jnp.bfloat16))
    added = lax.dot_general(
        jnp.concatenate(columns, axis=1),
        jnp.concatenate(planes, axis=1),
        NT,
        preferred_element_type=jnp.float32,
    )
    at = pl.ds(pl.multiple_of(block * ZB, ZB), rows)
    for c in range(channels):
        total[c, at, :] += added[c * rows : (c + 1) * rows]

    @pl.when(block == pl.num_programs(0) - 1)
    def _():
        width = total.shape[2]
        pick_row = lax.broadcasted_iota(jnp.int32, (HALO_ROWS, width), 0)
        pick_lane = lax.broadcasted_iota(jnp.int32, (HALO_ROWS, width), 1)
        pick = jnp.where(pick_lane == pick_row + tile_y, 1.0, 0.0).astype(jnp.bfloat16)
        for c in range(channels):
            total[c, NZ : NZ + 1, :] += total[c, 0:1, :]
            total[c, 1:2, :] += total[c, NZ + 1 : NZ + 2, :]
            whole = total[c, 1 : NZ + 1, :].astype(jnp.bfloat16)
            main_ref[c] = whole[:, :tile_y]
            rim_ref[c] = lax.dot_general(
                pick, whole, NT, preferred_element_type=jnp.float32
            ).astype(jnp.bfloat16)


def sample_kernel(
    tile_y, channels, own_ref, prev_ref, next_ref, field_ref, own_out, prev_out, next_out, padded
):
    block = pl.program_id(0)
    slots = own_ref.shape[2]
    width = field_ref.shape[2]

    @pl.when(block == 0)
    def _():
        for c in range(channels):
            padded[c, 16 : NZ + 16, :] = field_ref[c]
            padded[c, 0:16, :] = field_ref[c, NZ - 16 : NZ, :]
            padded[c, NZ + 16 : NZ + 32, :] = field_ref[c, 0:16, :]

    at = pl.ds(pl.multiple_of(block * ZB, ZB), 64)
    window = jnp.concatenate([padded[c, at, :] for c in range(channels)], axis=0)
    places = y_places(tile_y, slots)
    rows = 48
    zs = z_places(rows, 8, slots)
    unused = jnp.zeros((width - tile_y - HALO_ROWS, slots), jnp.float32)
    for group, (ref, out) in enumerate(
        ((own_ref, own_out), (prev_ref, prev_out), (next_ref, next_out))
    ):
        record = ref[0]
        gx, gy, gz, iy, iz = (record[i : i + 1] for i in range(5))
        weight_x = x_weight(group, gx)
        slope_x = x_slope(group, gx)
        weight_z = hat(zs, iz + gz)
        slope_z = step_pair(zs, iz - jnp.where(gz < 0.0, 1.0, 0.0))
        weight_y = hat(places, iy + gy)
        slope_y = step_pair(places, iy - jnp.where(gy < 0.0, 1.0, 0.0))
        weight_y = jnp.concatenate([weight_y, unused], axis=0).astype(jnp.bfloat16)
        slope_y = jnp.concatenate([slope_y, unused], axis=0).astype(jnp.bfloat16)
        values = lax.dot_general(window, weight_y, NN, preferred_element_type=jnp.float32)
        along_y = lax.dot_general(window, slope_y, NN, preferred_element_type=jnp.float32)
        lines = []
        mass_values = jnp.zeros((rows, slots), jnp.float32)
        mass_along = jnp.zeros((rows, slots), jnp.float32)
        for c in range(channels):
            mass = record[5 + c : 6 + c]
            here = values[c * 64 + 8 : c * 64 + 56]
            lines.append(weight_x * jnp.sum(here * weight_z, axis=0, keepdims=True))
            mass_values += mass * here
            mass_along += mass * along_y[c * 64 + 8 : c * 64 + 56]
        lines.append(slope_x * jnp.sum(mass_values * weight_z, axis=0, keepdims=True))
        lines.append(weight_x * jnp.sum(mass_along * weight_z, axis=0, keepdims=True))
        lines.append(weight_x * jnp.sum(mass_values * slope_z, axis=0, keepdims=True))
        lines.append(jnp.zeros((8 - len(lines), slots), jnp.float32))
        out[0] = jnp.concatenate(lines, axis=0)


def per_device(fractions, cell_index, weights, counts, smoothing, bias_values, observed, precision):
    slab_count = lax.axis_size("slab")
    pencil_count = lax.axis_size("pencil")
    tile_count = slab_count * pencil_count
    tile_y = NY // pencil_count
    z_blocks = NZ // ZB
    capacity = PART_DEV // (tile_count * z_blocks)
    channels = weights.shape[0]
    slots = tile_count * capacity
    low = jnp.bfloat16
    slot_rank = lax.broadcasted_iota(jnp.int32, (tile_count, z_blocks, capacity), 2)
    live_mask = (slot_rank < counts[0][:, :, None]).reshape(PART_DEV)
    masses = jnp.where(live_mask[None, :], weights, jnp.zeros((), low))
    fields = 5 + channels
    payload = jnp.concatenate(
        [(fractions - 0.5).astype(low), cell_index[1:3].astype(low), masses], axis=0
    )
    payload = jnp.transpose(
        payload.reshape(fields, tile_count, z_blocks * capacity), (1, 0, 2)
    )
    arrived = lax.all_to_all(payload, ("slab", "pencil"), split_axis=0, concat_axis=0, tiled=True)
    records = jnp.transpose(
        arrived.reshape(tile_count, fields, z_blocks, capacity), (2, 1, 0, 3)
    ).reshape(z_blocks, fields, slots)
    before = shifted(records, "slab", 1)
    after = shifted(records, "slab", -1)
    groups = [part.astype(jnp.float32) for part in (records, before, after)]

    record_spec = pl.BlockSpec((1, fields, slots), lambda b: (b, 0, 0))
    params = pltpu.CompilerParams(
        dimension_semantics=("arbitrary",), vmem_limit_bytes=48 * 1024 * 1024
    )
    span = tile_y + HALO_ROWS
    main, rim = pl.pallas_call(
        functools.partial(deposit_kernel, tile_y, channels),
        grid=(z_blocks,),
        in_specs=[record_spec] * 3,
        out_specs=[
            pl.BlockSpec((channels, NZ, tile_y), lambda b: (0, 0, 0)),
            pl.BlockSpec((channels, HALO_ROWS, NZ), lambda b: (0, 0, 0)),
        ],
        out_shape=[
            jax.ShapeDtypeStruct((channels, NZ, tile_y), low),
            jax.ShapeDtypeStruct((channels, HALO_ROWS, NZ), low),
        ],
        scratch_shapes=[pltpu.VMEM((channels, NZ + 16, span), jnp.float32)],
        compiler_params=params,
        name="deposit",
    )(*groups)
    to_last = shifted(rim[:, 0:1], "pencil", -1)
    to_first = shifted(rim[:, 1:2], "pencil", 1)
    edges = jnp.concatenate([to_first, to_last], axis=1)
    edge_row = lax.broadcasted_iota(jnp.int32, (2, tile_y), 0)
    edge_lane = lax.broadcasted_iota(jnp.int32, (2, tile_y), 1)
    edge_place = (edge_lane == edge_row * (tile_y - 1)).astype(low)
    density = (
        main.astype(jnp.float32)
        + jnp.einsum("ckz,ky->czy", edges, edge_place, preferred_element_type=jnp.float32)
    ).astype(low)

    kernels = jnp.stack([kernel_matrix(smoothing[c], NZ) for c in range(channels)])
    smooth_z = jnp.einsum(
        "cwz,czy->cwy", kernels, density, preferred_element_type=jnp.float32
    ).astype(low)
    lines = lax.all_to_all(smooth_z, "pencil", split_axis=1, concat_axis=2, tiled=True)
    summed = jnp.zeros((lines.shape[1], NY), jnp.float32)
    for c in range(channels):
        summed = summed + bias_values[c] * jnp.dot(
            lines[c], kernels[c], preferred_element_type=jnp.float32
        )
    model_field = summed.astype(low)[None]
    pull_field = (precision[0] * (summed - observed[0])).astype(low)
    returned_y = jnp.stack(
        [
            (
                bias_values[c]
                * jnp.dot(pull_field, kernels[c], preferred_element_type=jnp.float32)
            ).astype(low)
            for c in range(channels)
        ]
    )
    lines = lax.all_to_all(returned_y, "pencil", split_axis=2, concat_axis=1, tiled=True)
    adjoint = jnp.einsum(
        "cwz,czy->cwy", kernels, lines, preferred_element_type=jnp.float32
    ).astype(low)
    edges = jnp.einsum(
        "ky,czy->ckz", edge_place, adjoint, preferred_element_type=jnp.float32
    ).astype(low)
    below = shifted(edges[:, 1:2], "pencil", 1)
    above = shifted(edges[:, 0:1], "pencil", -1)
    width = -(-span // 128) * 128
    rim_row = lax.broadcasted_iota(jnp.int32, (2, width), 0)
    rim_lane = lax.broadcasted_iota(jnp.int32, (2, width), 1)
    rim_place = (rim_lane == rim_row + tile_y).astype(low)
    field = (
        jnp.pad(adjoint, ((0, 0), (0, 0), (0, width - tile_y))).astype(jnp.float32)
        + jnp.einsum(
            "ckz,ky->czy",
            jnp.concatenate([below, above], axis=1),
            rim_place,
            preferred_element_type=jnp.float32,
        )
    ).astype(low)

    result_spec = pl.BlockSpec((1, 8, slots), lambda b: (b, 0, 0))
    mine, for_before, for_after = pl.pallas_call(
        functools.partial(sample_kernel, tile_y, channels),
        grid=(z_blocks,),
        in_specs=[record_spec] * 3
        + [pl.BlockSpec((channels, NZ, width), lambda b: (0, 0, 0))],
        out_specs=[result_spec] * 3,
        out_shape=[jax.ShapeDtypeStruct((z_blocks, 8, slots), jnp.float32)] * 3,
        scratch_shapes=[pltpu.VMEM((channels, NZ + 32, width), low)],
        compiler_params=params,
        name="sample",
    )(*groups, field)
    gathered = (
        mine
        + shifted(for_before.astype(low), "slab", -1).astype(jnp.float32)
        + shifted(for_after.astype(low), "slab", 1).astype(jnp.float32)
    ).astype(low)
    outgoing = jnp.transpose(
        gathered.reshape(z_blocks, 8, tile_count, capacity), (2, 1, 0, 3)
    ).reshape(tile_count, 8, z_blocks * capacity)
    came_back = lax.all_to_all(
        outgoing, ("slab", "pencil"), split_axis=0, concat_axis=0, tiled=True
    )
    particle_grads = jnp.transpose(came_back, (1, 0, 2)).reshape(8, PART_DEV)[: channels + 3]
    particle_grads = jnp.where(live_mask[None, :], particle_grads.astype(jnp.float32), 0.0)
    return (particle_grads, model_field)


def solution(mesh):
    return jax.shard_map(
        per_device,
        mesh=mesh,
        in_specs=(
            P(None, ("slab", "pencil")),
            P(None, ("slab", "pencil")),
            P(None, ("slab", "pencil")),
            P(("slab", "pencil"), None, None),
            P(),
            P(),
            P("slab", "pencil", None),
            P("slab", "pencil", None),
        ),
        out_specs=(P(None, ("slab", "pencil")), P("slab", "pencil", None)),
        check_vma=False,
    )
```

```python
import functools

import jax
import jax.numpy as jnp
from jax import lax
from jax.experimental import pallas as pl
from jax.experimental.pallas import tpu as pltpu
from jax.sharding import PartitionSpec as P

NY = 1024
NZ = 1024
ZB = 32
PART_DEV = 16384
HALO_ROWS = 8
NT = (((1,), (1,)), ((), ()))
NN = (((1,), (0,)), ((), ()))


def shifted(value, axis, step):
    count = lax.axis_size(axis)
    return lax.ppermute(value, axis, [(i, (i + step) % count) for i in range(count)])


def kernel_matrix(breadth, extent):
    places = jnp.arange(extent, dtype=jnp.int32)
    distance = jnp.abs(places[:, None] - places[None, :])
    distance = jnp.minimum(distance, extent - distance).astype(jnp.float32)
    profile = jnp.exp(-distance * distance / (2.0 * breadth * breadth)) / jnp.sqrt(breadth)
    return (profile + jnp.where(distance == 0.0, 1.0, 0.0)).astype(jnp.bfloat16)


def y_places(tile_y, slots):
    main = lax.broadcasted_iota(jnp.int32, (tile_y, slots), 0).astype(jnp.float32)
    rim = lax.broadcasted_iota(jnp.int32, (HALO_ROWS, slots), 0)
    rim = jnp.where(rim == 0, -1.0, jnp.where(rim == 1, float(tile_y), -1000.0))
    return jnp.concatenate([main, rim], axis=0)


def z_places(rows, below, slots):
    return (lax.broadcasted_iota(jnp.int32, (rows, slots), 0) - below).astype(jnp.float32)


def hat(places, position):
    return jnp.maximum(1.0 - jnp.abs(places - position), 0.0)


def step_pair(places, lower):
    relative = places - lower
    return jnp.where(relative == 1.0, 1.0, jnp.where(relative == 0.0, -1.0, 0.0))


def x_weight(group, gx):
    if group == 0:
        return 1.0 - jnp.abs(gx)
    return jnp.maximum(gx if group == 1 else -gx, 0.0)


def x_slope(group, gx):
    falling = gx < 0.0
    if group == 0:
        return jnp.where(falling, 1.0, -1.0)
    if group == 1:
        return jnp.where(falling, 0.0, 1.0)
    return jnp.where(falling, -1.0, 0.0)


def deposit_kernel(tile_y, channels, own_ref, prev_ref, next_ref, main_ref, rim_ref, total):
    block = pl.program_id(0)
    rows = ZB + 8
    slots = own_ref.shape[2]

    @pl.when(block == 0)
    def _():
        total[...] = jnp.zeros_like(total)

    places = y_places(tile_y, slots)
    zs = z_places(rows, 1, slots)
    columns = []
    planes = []
    for group, ref in enumerate((own_ref, prev_ref, next_ref)):
        record = ref[0]
        gx, gy, gz, iy, iz = (record[i : i + 1] for i in range(5))
        along_z = hat(zs, iz + gz) * x_weight(group, gx)
        columns.append(
            jnp.concatenate(
                [along_z * record[5 + c : 6 + c] for c in range(channels)], axis=0
            ).astype(jnp.bfloat16)
        )
        planes.append(hat(places, iy + gy).astype(jnp.bfloat16))
    added = lax.dot_general(
        jnp.concatenate(columns, axis=1),
        jnp.concatenate(planes, axis=1),
        NT,
        preferred_element_type=jnp.float32,
    )
    at = pl.ds(pl.multiple_of(block * ZB, ZB), rows)
    for c in range(channels):
        total[c, at, :] += added[c * rows : (c + 1) * rows]

    @pl.when(block == pl.num_programs(0) - 1)
    def _():
        width = total.shape[2]
        pick_row = lax.broadcasted_iota(jnp.int32, (HALO_ROWS, width), 0)
        pick_lane = lax.broadcasted_iota(jnp.int32, (HALO_ROWS, width), 1)
        pick = jnp.where(pick_lane == pick_row + tile_y, 1.0, 0.0).astype(jnp.bfloat16)
        for c in range(channels):
            total[c, NZ : NZ + 1, :] += total[c, 0:1, :]
            total[c, 1:2, :] += total[c, NZ + 1 : NZ + 2, :]
            whole = total[c, 1 : NZ + 1, :].astype(jnp.bfloat16)
            main_ref[c] = whole[:, :tile_y]
            rim_ref[c] = lax.dot_general(
                pick, whole, NT, preferred_element_type=jnp.float32
            ).astype(jnp.bfloat16)


def sample_kernel(
    tile_y, channels, own_ref, prev_ref, next_ref, field_ref, own_out, prev_out, next_out, padded
):
    block = pl.program_id(0)
    slots = own_ref.shape[2]
    width = field_ref.shape[2]

    @pl.when(block == 0)
    def _():
        for c in range(channels):
            padded[c, 16 : NZ + 16, :] = field_ref[c]
            padded[c, 0:16, :] = field_ref[c, NZ - 16 : NZ, :]
            padded[c, NZ + 16 : NZ + 32, :] = field_ref[c, 0:16, :]

    at = pl.ds(pl.multiple_of(block * ZB, ZB), 64)
    window = jnp.concatenate([padded[c, at, :] for c in range(channels)], axis=0)
    places = y_places(tile_y, slots).astype(jnp.bfloat16)
    rows = 48
    zs = z_places(rows, 8, slots)
    unused = jnp.zeros((width - tile_y - HALO_ROWS, slots), jnp.bfloat16)
    for group, (ref, out) in enumerate(
        ((own_ref, own_out), (prev_ref, prev_out), (next_ref, next_out))
    ):
        record = ref[0]
        gx, gy, gz, iy, iz = (record[i : i + 1] for i in range(5))
        weight_x = x_weight(group, gx)
        slope_x = x_slope(group, gx)
        weight_z = hat(zs, iz + gz)
        slope_z = step_pair(zs, iz - jnp.where(gz < 0.0, 1.0, 0.0))
        lower = iy - jnp.where(gy < 0.0, 1.0, 0.0)
        share = gy + (iy - lower)
        at_lower = places == lower.astype(jnp.bfloat16)
        at_upper = places == (lower + 1.0).astype(jnp.bfloat16)
        none = jnp.zeros((), jnp.bfloat16)
        one = jnp.ones((), jnp.bfloat16)
        weight_y = jnp.where(
            at_lower,
            (1.0 - share).astype(jnp.bfloat16),
            jnp.where(at_upper, share.astype(jnp.bfloat16), none),
        )
        slope_y = jnp.where(at_lower, -one, jnp.where(at_upper, one, none))
        weight_y = jnp.concatenate([weight_y, unused], axis=0)
        slope_y = jnp.concatenate([slope_y, unused], axis=0)
        values = lax.dot_general(window, weight_y, NN, preferred_element_type=jnp.float32)
        along_y = lax.dot_general(window, slope_y, NN, preferred_element_type=jnp.float32)
        lines = []
        mass_values = jnp.zeros((rows, slots), jnp.float32)
        mass_along = jnp.zeros((rows, slots), jnp.float32)
        for c in range(channels):
            mass = record[5 + c : 6 + c]
            here = values[c * 64 + 8 : c * 64 + 56]
            lines.append(weight_x * jnp.sum(here * weight_z, axis=0, keepdims=True))
            mass_values += mass * here
            mass_along += mass * along_y[c * 64 + 8 : c * 64 + 56]
        lines.append(slope_x * jnp.sum(mass_values * weight_z, axis=0, keepdims=True))
        lines.append(weight_x * jnp.sum(mass_along * weight_z, axis=0, keepdims=True))
        lines.append(weight_x * jnp.sum(mass_values * slope_z, axis=0, keepdims=True))
        lines.append(jnp.zeros((8 - len(lines), slots), jnp.float32))
        out[0] = jnp.concatenate(lines, axis=0)


def smooth_kernel(kernel_ref, density_ref, out_ref):
    smoothed = jnp.dot(kernel_ref[0], density_ref[0], preferred_element_type=jnp.float32)
    parts, _, tall, _ = out_ref.shape
    for part in range(parts):
        out_ref[part, 0] = smoothed[part * tall : (part + 1) * tall].astype(jnp.bfloat16)


def adjoint_kernel(kernel_ref, lines_ref, out_ref):
    lines = jnp.concatenate([lines_ref[part, 0] for part in range(lines_ref.shape[0])], axis=0)
    out_ref[0] = jnp.dot(kernel_ref[0], lines, preferred_element_type=jnp.float32).astype(
        jnp.bfloat16
    )


def pull_kernel(
    channels, bias_ref, kernel_ref, lines_ref, seen_ref, precision_ref, model_ref, back_ref, summed, pull
):
    step = pl.program_id(0)
    parts, _, _, wide = lines_ref.shape

    @pl.when(step == 0)
    def _():
        summed[...] = jnp.zeros_like(summed)

    @pl.when(step < channels)
    def _():
        lines = jnp.concatenate([lines_ref[part, 0] for part in range(parts)], axis=1)
        summed[...] += bias_ref[step] * jnp.dot(
            lines, kernel_ref[0], preferred_element_type=jnp.float32
        )

    @pl.when(step == channels - 1)
    def _():
        model_ref[...] = summed[...].astype(jnp.bfloat16)
        pull[...] = (precision_ref[...] * (summed[...] - seen_ref[...])).astype(jnp.bfloat16)

    @pl.when(step >= channels)
    def _():
        back = bias_ref[2 * channels - 1 - step] * jnp.dot(
            pull[...], kernel_ref[0], preferred_element_type=jnp.float32
        )
        for part in range(parts):
            back_ref[part, 0] = back[:, part * wide : (part + 1) * wide].astype(jnp.bfloat16)


def per_device(fractions, cell_index, weights, counts, smoothing, bias_values, observed, precision):
    slab_count = lax.axis_size("slab")
    pencil_count = lax.axis_size("pencil")
    tile_count = slab_count * pencil_count
    tile_y = NY // pencil_count
    z_blocks = NZ // ZB
    capacity = PART_DEV // (tile_count * z_blocks)
    channels = weights.shape[0]
    slots = tile_count * capacity
    low = jnp.bfloat16
    slot_rank = lax.broadcasted_iota(jnp.int32, (tile_count, z_blocks, capacity), 2)
    live_mask = (slot_rank < counts[0][:, :, None]).reshape(PART_DEV)
    masses = jnp.where(live_mask[None, :], weights, jnp.zeros((), low))
    fields = 5 + channels
    payload = jnp.concatenate(
        [(fractions - 0.5).astype(low), cell_index[1:3].astype(low), masses], axis=0
    )
    payload = jnp.transpose(
        payload.reshape(fields, tile_count, z_blocks * capacity), (1, 0, 2)
    )
    arrived = lax.all_to_all(payload, ("slab", "pencil"), split_axis=0, concat_axis=0, tiled=True)
    records = jnp.transpose(
        arrived.reshape(tile_count, fields, z_blocks, capacity), (2, 1, 0, 3)
    ).reshape(z_blocks, fields, slots)
    before = shifted(records, "slab", 1)
    after = shifted(records, "slab", -1)
    groups = [part.astype(jnp.float32) for part in (records, before, after)]

    record_spec = pl.BlockSpec((1, fields, slots), lambda b: (b, 0, 0))
    params = pltpu.CompilerParams(
        dimension_semantics=("arbitrary",), vmem_limit_bytes=48 * 1024 * 1024
    )
    span = tile_y + HALO_ROWS
    main, rim = pl.pallas_call(
        functools.partial(deposit_kernel, tile_y, channels),
        grid=(z_blocks,),
        in_specs=[record_spec] * 3,
        out_specs=[
            pl.BlockSpec((channels, NZ, tile_y), lambda b: (0, 0, 0)),
            pl.BlockSpec((channels, HALO_ROWS, NZ), lambda b: (0, 0, 0)),
        ],
        out_shape=[
            jax.ShapeDtypeStruct((channels, NZ, tile_y), low),
            jax.ShapeDtypeStruct((channels, HALO_ROWS, NZ), low),
        ],
        scratch_shapes=[pltpu.VMEM((channels, NZ + 16, span), jnp.float32)],
        compiler_params=params,
        name="deposit",
    )(*groups)
    to_last = shifted(rim[:, 0:1], "pencil", -1)
    to_first = shifted(rim[:, 1:2], "pencil", 1)
    edges = jnp.concatenate([to_first, to_last], axis=1)
    edge_row = lax.broadcasted_iota(jnp.int32, (2, tile_y), 0)
    edge_lane = lax.broadcasted_iota(jnp.int32, (2, tile_y), 1)
    edge_place = (edge_lane == edge_row * (tile_y - 1)).astype(low)
    density = (
        main.astype(jnp.float32)
        + jnp.einsum("ckz,ky->czy", edges, edge_place, preferred_element_type=jnp.float32)
    ).astype(low)

    kernels = jnp.stack([kernel_matrix(smoothing[c], NZ) for c in range(channels)])
    tall = NZ // pencil_count
    kernel_spec = pl.BlockSpec((1, NZ, NZ), lambda c: (c, 0, 0))
    field_spec = pl.BlockSpec((1, NZ, tile_y), lambda c: (c, 0, 0))
    parts_spec = pl.BlockSpec((pencil_count, 1, tall, tile_y), lambda c: (0, c, 0, 0))
    parts_shape = jax.ShapeDtypeStruct((pencil_count, channels, tall, tile_y), low)
    smooth_z = pl.pallas_call(
        smooth_kernel,
        grid=(channels,),
        in_specs=[kernel_spec, field_spec],
        out_specs=parts_spec,
        out_shape=parts_shape,
        compiler_params=params,
        name="smooth",
    )(kernels, density)
    lines = lax.all_to_all(smooth_z, "pencil", split_axis=0, concat_axis=0, tiled=True)
    last = channels - 1

    def turn(step):
        return jnp.where(step < channels, step, 2 * channels - 1 - step)

    whole_spec = pl.BlockSpec((tall, NY), lambda s: (0, 0))
    model_field, returned_y = pl.pallas_call(
        functools.partial(pull_kernel, channels),
        grid=(2 * channels,),
        in_specs=[
            pl.BlockSpec(memory_space=pltpu.SMEM),
            pl.BlockSpec((1, NY, NY), lambda s: (turn(s), 0, 0)),
            pl.BlockSpec(
                (pencil_count, 1, tall, tile_y), lambda s: (0, jnp.minimum(s, last), 0, 0)
            ),
            whole_spec,
            whole_spec,
        ],
        out_specs=[
            whole_spec,
            pl.BlockSpec(
                (pencil_count, 1, tall, tile_y),
                lambda s: (0, jnp.minimum(2 * channels - 1 - s, last), 0, 0),
            ),
        ],
        out_shape=[jax.ShapeDtypeStruct((tall, NY), low), parts_shape],
        scratch_shapes=[pltpu.VMEM((tall, NY), jnp.float32), pltpu.VMEM((tall, NY), low)],
        compiler_params=params,
        name="pull",
    )(bias_values, kernels, lines, observed[0], precision[0])
    model_field = model_field[None]
    lines = lax.all_to_all(returned_y, "pencil", split_axis=0, concat_axis=0, tiled=True)
    adjoint = pl.pallas_call(
        adjoint_kernel,
        grid=(channels,),
        in_specs=[kernel_spec, parts_spec],
        out_specs=field_spec,
        out_shape=jax.ShapeDtypeStruct((channels, NZ, tile_y), low),
        compiler_params=params,
        name="adjoint",
    )(kernels, lines)
    edges = jnp.einsum(
        "ky,czy->ckz", edge_place, adjoint, preferred_element_type=jnp.float32
    ).astype(low)
    below = shifted(edges[:, 1:2], "pencil", 1)
    above = shifted(edges[:, 0:1], "pencil", -1)
    width = -(-span // 128) * 128
    rim_row = lax.broadcasted_iota(jnp.int32, (2, width), 0)
    rim_lane = lax.broadcasted_iota(jnp.int32, (2, width), 1)
    rim_place = (rim_lane == rim_row + tile_y).astype(low)
    field = (
        jnp.pad(adjoint, ((0, 0), (0, 0), (0, width - tile_y))).astype(jnp.float32)
        + jnp.einsum(
            "ckz,ky->czy",
            jnp.concatenate([below, above], axis=1),
            rim_place,
            preferred_element_type=jnp.float32,
        )
    ).astype(low)

    result_spec = pl.BlockSpec((1, 8, slots), lambda b: (b, 0, 0))
    mine, for_before, for_after = pl.pallas_call(
        functools.partial(sample_kernel, tile_y, channels),
        grid=(z_blocks,),
        in_specs=[record_spec] * 3
        + [pl.BlockSpec((channels, NZ, width), lambda b: (0, 0, 0))],
        out_specs=[result_spec] * 3,
        out_shape=[jax.ShapeDtypeStruct((z_blocks, 8, slots), jnp.float32)] * 3,
        scratch_shapes=[pltpu.VMEM((channels, NZ + 32, width), low)],
        compiler_params=params,
        name="sample",
    )(*groups, field)
    gathered = (
        mine
        + shifted(for_before.astype(low), "slab", -1).astype(jnp.float32)
        + shifted(for_after.astype(low), "slab", 1).astype(jnp.float32)
    ).astype(low)
    outgoing = jnp.transpose(
        gathered.reshape(z_blocks, 8, tile_count, capacity), (2, 1, 0, 3)
    ).reshape(tile_count, 8, z_blocks * capacity)
    came_back = lax.all_to_all(
        outgoing, ("slab", "pencil"), split_axis=0, concat_axis=0, tiled=True
    )
    particle_grads = jnp.transpose(came_back, (1, 0, 2)).reshape(8, PART_DEV)[: channels + 3]
    particle_grads = jnp.where(live_mask[None, :], particle_grads.astype(jnp.float32), 0.0)
    return (particle_grads, model_field)


def solution(mesh):
    return jax.shard_map(
        per_device,
        mesh=mesh,
        in_specs=(
            P(None, ("slab", "pencil")),
            P(None, ("slab", "pencil")),
            P(None, ("slab", "pencil")),
            P(("slab", "pencil"), None, None),
            P(),
            P(),
            P("slab", "pencil", None),
            P("slab", "pencil", None),
        ),
        out_specs=(P(None, ("slab", "pencil")), P("slab", "pencil", None)),
        check_vma=False,
    )
```
